32 devices in a mesh: rep: 2 (over x), seq: 16 (over z, y, core).
Axes of the slice: x: 2, y: 2, z: 4, core: 2. Of those that a mesh axis runs over, the one named last changes fastest.
Arguments:
- tokens: bfloat16 [256, 12288], P('rep', 'seq'), parts along dimension 0, may hold values from -6 to 6
- w_query: bfloat16 [12288, 12288], P(None, 'seq'), may hold values from -0.0546875 to 0.0546875
- w_key_value: bfloat16 [12288, 2048], P('seq'), may hold values from -0.0546875 to 0.0546875
- w_out: bfloat16 [12288, 12288], P('seq'), may hold values from -0.078125 to 0.078125
- cache_keys: bfloat16 [16384, 1024], P(('rep', 'seq')), parts along dimension 0, as said below
- cache_values: bfloat16 [16384, 1024], P(('rep', 'seq')), parts along dimension 0, may hold values from -6 to 6
- lengths: int32 [32], P(('rep', 'seq')), parts along dimension 0, may hold values from 128 to 512, as said below
- offset: int32 [2], P('rep'), parts along dimension 0, may hold values from 6144 to 8192
Outputs:
- mixed: bfloat16 [256, 12288], P('rep', 'seq'), parts along dimension 0
The draws below stay inside these ranges and needn't reach their ends.
There are 2 independent parts, one for each index of `rep`. The reference program is written for one: setup_inputs(seed, part) draws one part's arguments, and reference() takes and returns one part's arrays. A program takes and returns all parts, laid end to end along the dimension named above; an argument that names none is the same for every part. Nothing has to cross between parts.
Inputs may be any that keep to these rules, and one draw needn't show every extreme that they name: `lengths`: every block of 512 slots has between 128 and 512 filled slots; some block is full. `cache_keys`: entries lie within -100 and 100.
All inputs are finite; a program needn't handle non-finite values.
Results may differ from the reference program's by a relative error of at most 0.0087.
Values may be sent and summed in bfloat16 or wider, within the bound.
A program may use at most 192 MiB of HBM per device.

```python
import jax
import jax.numpy as jnp
from jax import lax

D = 12288
HQ = 96
HK = 8
E = 128
Q = 128
L_DEV = 512
CACHE = 8192
N_SEQ = 16


def draw_lengths(key, part):
    key = jax.random.fold_in(key, 5)
    first_key, second_key = jax.random.split(key)
    filled = jax.random.randint(first_key, (N_SEQ,), L_DEV // 4, L_DEV + 1)
    chosen = jax.random.randint(second_key, (), 0, N_SEQ)
    return jnp.where(jnp.arange(N_SEQ) == chosen, L_DEV, filled).astype(jnp.int32)


def draw_cache_keys(key, part):
    key = jax.random.fold_in(key, 11)
    entries = jax.random.normal(key, (CACHE, HK * E), jnp.float32)
    return entries.astype(jnp.bfloat16)


def with_spikes(array, rng, source, target, blocks, factor):
    def block_of(dim):
        return (jnp.arange(array.shape[dim]) // (array.shape[dim] // blocks)).reshape((-1,) + (1,) * (array.ndim - 1 - dim))

    one_side = jax.random.permutation(rng, blocks)[block_of(target)]
    far = (block_of(target) + blocks // 2) % blocks
    return jnp.where((block_of(source) == one_side) | (block_of(source) == far), factor * array, array)


def levels(key, shape, cuts, smallest, largest):
    level = 1.0
    for position, shards_of in cuts:
        heights = jax.random.uniform(jax.random.fold_in(jax.random.fold_in(key, 6), position), (shards_of,), jnp.float32, smallest / len(cuts), largest / len(cuts))
        level = level * jnp.repeat(jnp.exp(heights), shape[position] // shards_of).reshape((-1,) + (1,) * (len(shape) - 1 - position))
    return level


def centred(stream_key, shape, deviation, limit, pieces=(), held_as=jnp.bfloat16):
    factor_of = levels(stream_key, shape, pieces, -0.22, 0.18) if pieces else 1.0
    result = jax.random.normal(stream_key, shape, jnp.float32) * deviation * factor_of
    return jnp.minimum(jnp.maximum(result, -limit), limit).astype(held_as)


def heavy_noise(rng, shape, deviation, limit, cuts, heavy, held_as=jnp.bfloat16):
    values = deviation * jax.random.normal(rng, shape, jnp.float32)
    if cuts:
        values = values * levels(rng, shape, cuts, -0.22, 0.18)
    return jnp.clip(with_spikes(values, jax.random.fold_in(rng, 3), *heavy), -limit, limit).astype(held_as)


def setup_inputs(seed: int = 0, part: int = 0) -> dict:
    arg_keys = jax.random.split(jax.random.key(seed), 9)
    own_keys = jax.random.split(jax.random.fold_in(arg_keys[8], part), 9)
    tokens = centred(own_keys[0], (Q, D), 1.0, 6.0, ((1, 16),))
    w_query = centred(arg_keys[1], (D, HQ * E), D ** -0.5, 0.0546875, ((1, 16),))
    w_key_value = centred(arg_keys[2], (D, 2 * HK * E), D ** -0.5, 0.0546875, ((0, 16),))
    w_out = heavy_noise(arg_keys[3], (HQ * E, D), (HQ * E) ** -0.5, 0.078125, ((0, 16),), (0, 1, 16, 2.0))
    cache_keys = draw_cache_keys(jax.random.fold_in(jax.random.fold_in(arg_keys[8], part), 71), part)
    cache_values = centred(own_keys[5], (CACHE, HK * E), 1.0, 6.0, ((0, 16),))
    lengths = draw_lengths(jax.random.fold_in(jax.random.fold_in(arg_keys[8], part), 71), part)
    offset = jax.random.randint(own_keys[7], (1,), 3 * CACHE // 4, CACHE + 1).astype(jnp.int32)
    return dict(tokens=tokens, w_query=w_query, w_key_value=w_key_value, w_out=w_out, cache_keys=cache_keys, cache_values=cache_values, lengths=lengths, offset=offset)


NEGATIVE_FILL = -1.0e30


def reference(tokens, w_query, w_key_value, w_out, cache_keys, cache_values, lengths, offset):
    span_rows = tokens.shape[0]
    kv_columns = HK * E
    group_size = HQ // HK
    queries = (jnp.dot(tokens, w_query, preferred_element_type=jnp.float32) * (E ** -0.5)).astype(jnp.bfloat16)
    fresh_rows = jnp.dot(tokens, w_key_value, preferred_element_type=jnp.float32).astype(jnp.bfloat16)
    all_keys = jnp.concatenate([cache_keys, fresh_rows[:, :kv_columns]], 0)
    all_values = jnp.concatenate([cache_values, fresh_rows[:, kv_columns:]], 0)
    cache_slot = jnp.arange(CACHE, dtype=jnp.int32)
    block_fill = lengths[(cache_slot // L_DEV).astype(jnp.int32)]
    cache_live = ((cache_slot % L_DEV) < block_fill) & (cache_slot < offset[0])
    token_index = jnp.arange(span_rows, dtype=jnp.int32)
    causal = token_index[None, :] <= token_index[:, None]
    visible = jnp.concatenate([jnp.broadcast_to(cache_live[None, :], (span_rows, CACHE)), causal], 1)
    query_heads = queries.reshape(span_rows, HK, group_size, E).transpose(1, 0, 2, 3)
    key_heads = all_keys.reshape(-1, HK, E).transpose(1, 0, 2)
    value_heads = all_values.reshape(-1, HK, E).transpose(1, 0, 2)

    def one_head(operands):
        query_group, key_group, value_group = operands
        scores = jnp.einsum('qge,pe->gqp', query_group.astype(jnp.float32), key_group.astype(jnp.float32))
        scores = jnp.where(visible[None], scores, NEGATIVE_FILL)
        highest = jnp.max(scores, axis=-1, keepdims=True)
        exponent = jnp.where(visible[None], jnp.exp(scores - highest), 0.0)
        totals = jnp.sum(exponent, axis=-1)
        weights = exponent.astype(jnp.bfloat16)
        numerator = jnp.einsum('gqp,pe->qge', weights.astype(jnp.float32), value_group.astype(jnp.float32))
        return numerator / totals.T[:, :, None]

    attended = lax.map(one_head, (query_heads, key_heads, value_heads))
    attention = attended.transpose(1, 0, 2, 3).reshape(span_rows, HQ * E).astype(jnp.bfloat16)
    return jnp.dot(attention, w_out, preferred_element_type=jnp.float32).astype(jnp.bfloat16)
```

```python
import jax
import jax.numpy as jnp
from jax import lax
from jax.experimental import pallas as pl
from jax.experimental.pallas import tpu as pltpu
from jax.sharding import PartitionSpec as P

E = 128
MASK_ROWS = 16


NEGATIVE_FILL = -1e30


def kernel(tokens, w_query, w_key_value, w_out, cache_keys, cache_values, lengths, offset, out,
           tok, weights, w_kv, stage, kv, mine, theirs, fresh_out, fresh_in, fresh, projected, query,
           high, total, attended, attention, first_out, first_in, second_out, second_in, third_out, third_in,
           load_sem, weight_sem, tok_send, tok_recv, kv_send, kv_recv, kv_pass, pair_send, pair_recv,
           fresh_send, fresh_recv, share_send, share_recv, one_send, one_recv, two_send, two_recv,
           three_send, three_recv):
    rows, width = tokens.shape
    slots = cache_keys.shape[0]
    n_z = tok.shape[0] // 4
    chips = 2 * n_z
    half = w_kv.shape[1] // 2
    group = width // E
    f32, bf16 = jnp.float32, jnp.bfloat16
    me = lax.axis_index("seq")
    core = lax.rem(me, 2)
    chip = me // 2
    y = lax.rem(chip, 2)
    z = chip // 2
    other = me + 1 - 2 * core

    def index(zz, yy, cc):
        return (zz * 2 + yy) * 2 + cc

    def shifted(kz):
        return lax.rem(z + kz, n_z)

    y_peer = index(z, 1 - y, core)

    def remote(src, dst, send, recv, peer):
        return pltpu.make_async_remote_copy(
            src_ref=src, dst_ref=dst, send_sem=send, recv_sem=recv,
            device_id={"seq": peer}, device_id_type=pl.DeviceIdType.MESH)

    own_tokens = pltpu.make_async_copy(tokens, tok.at[me], load_sem.at[0])
    own_tokens.start()
    load_kv = pltpu.make_async_copy(w_key_value, w_kv, load_sem.at[1])
    load_kv.start()

    def query_weight(i):
        return pltpu.make_async_copy(
            w_query.at[pl.ds(pl.multiple_of(i * width, width), width), :], weights.at[i], weight_sem.at[i])

    def out_weight(i):
        return pltpu.make_async_copy(
            w_out.at[:, pl.ds(pl.multiple_of(i * width, width), width)], weights.at[i], weight_sem.at[i])

    stage_loads = []
    for head in range(chips):
        columns = pl.ds(head * E, E)
        for part, cache in enumerate((cache_keys, cache_values)):
            stage_loads.append(pltpu.make_async_copy(
                cache.at[:, columns], stage.at[head, pl.ds(part * slots, slots), :],
                load_sem.at[2 + 2 * head + part]))
    own_columns = pl.ds(pl.multiple_of(chip * E, E), E)
    own_loads = [
        pltpu.make_async_copy(cache.at[:, own_columns], kv.at[me, pl.ds(part * slots, slots), :],
                              load_sem.at[2 + 2 * chips + part])
        for part, cache in enumerate((cache_keys, cache_values))]
    for load in stage_loads + own_loads:
        load.start()

    @pl.loop(0, tok.shape[0])
    def _(i):
        query_weight(i).start()

    barrier = pltpu.get_barrier_semaphore()
    peers = [index(shifted(kz), yy, core) for kz in range(n_z) for yy in (y, 1 - y)][1:] + [other]
    for peer in peers:
        pl.semaphore_signal(barrier, inc=1, device_id={"seq": peer}, device_id_type=pl.DeviceIdType.MESH)
    pl.semaphore_wait(barrier, len(peers))

    def tok_copy(i, send, peer):
        return remote(tok.at[i], tok.at[i], tok_send.at[send], tok_recv.at[i], peer)

    own_tokens.wait()
    sends = []
    for kz in range(1, n_z):
        sends.append(tok_copy(me, kz - 1, index(shifted(kz), y, core)))
    sends.append(tok_copy(me, n_z - 1, y_peer))
    sends.append(tok_copy(me, 2 * n_z - 1, other))
    for copy in sends:
        copy.start()

    lane = lax.broadcasted_iota(jnp.int32, (MASK_ROWS, E), 0) * E + lax.broadcasted_iota(jnp.int32, (MASK_ROWS, E), 1)
    seen = (lane < lengths[0]) & (me * slots + lane < offset[0])
    bias = jnp.where(seen, 0.0, NEGATIVE_FILL).astype(bf16)
    for head in range(chips):
        stage[head, pl.ds(2 * slots, MASK_ROWS), :] = bias
    kv[me, pl.ds(2 * slots, MASK_ROWS), :] = bias

    load_kv.wait()
    for part in range(2):
        product = jnp.dot(tok[me], w_kv[:, pl.ds(part * half, half)], preferred_element_type=f32)

        @pl.when(core == part)
        def _():
            mine[...] = product

        @pl.when(core != part)
        def _():
            theirs[0] = product

    pair = remote(theirs.at[0], theirs.at[1], pair_send, pair_recv, other)
    pair.start()

    projected[...] = jnp.zeros_like(projected)

    def project(i):
        query_weight(i).wait()
        projected[...] += jnp.dot(tok[i], weights[i], preferred_element_type=f32)
        out_weight(i).start()

    project(me)

    pair.wait_recv()
    for head in range(chips):
        fresh_out[head] = (mine[:, head * E:(head + 1) * E] + theirs[1, :, head * E:(head + 1) * E]).astype(bf16)
    fresh_copies = []
    for k in range(1, chips):
        to = index(shifted(k // 2), lax.rem(y + k, 2), 0) // 2
        copy = remote(fresh_out.at[to], fresh_in.at[chip], fresh_send.at[k], fresh_recv.at[chip], to * 2 + core)
        copy.start()
        fresh_copies.append(copy)

    def fwd(i, kz, second):
        if not second:
            on = tok_copy(i, n_z - 1 + kz, y_peer)
            on.start()
            sends.append(on)
        on = tok_copy(i, 2 * n_z - 1 + 2 * kz + second, other)
        on.start()
        sends.append(on)

    def tok_wait(i):
        tok_copy(i, 0, other).wait_recv()

    near = [1, n_z - 1] + list(range(2, n_z - 1))
    for kz in near:
        i = index(shifted(kz), y, core)
        tok_wait(i)
        fwd(i, kz, 0)

    for load in stage_loads + own_loads:
        load.wait()

    def kv_to(k):
        to = index(shifted(k // 2), lax.rem(y + k, 2), 0) // 2
        return remote(stage.at[to], kv.at[me], kv_send.at[k], kv_recv.at[me], to * 2 + core)

    def kv_on(i, k):
        return remote(kv.at[i], kv.at[i], kv_pass.at[k], kv_recv.at[i], other)

    def kv_wait(i):
        kv_on(i, 0).wait_recv()

    for k in range(1, chips):
        kv_to(k).start()
    kv_on(me, 0).start()

    for kz in [0] + near:
        i = index(shifted(kz), 1 - y, core)
        tok_wait(i)
        fwd(i, kz, 1)

    @pl.loop(1, n_z)
    def _(kz):
        project(index(shifted(kz), y, core))

    @pl.loop(0, n_z)
    def _(kz):
        project(index(shifted(kz), 1 - y, core))

    @pl.loop(0, chips)
    def _(k):
        i = index(shifted(k // 2), lax.rem(y + k, 2), 1 - core)
        tok_wait(i)
        project(i)

    for head in range(group):
        query[head] = (projected[:, head * E:(head + 1) * E] * E ** (-0.5)).astype(bf16)

    new_rows = fresh_out[chip].astype(f32)
    for k in range(1, chips):
        source = index(shifted(k // 2), lax.rem(y + k, 2), 0) // 2
        remote(fresh_out.at[source], fresh_in.at[source], fresh_send.at[0], fresh_recv.at[source], other).wait_recv()
        new_rows += fresh_in[source].astype(f32)
    fresh[core] = new_rows.astype(bf16)
    share = remote(fresh.at[core], fresh.at[core], share_send, share_recv.at[core], other)
    share.start()

    high[...] = jnp.full_like(high, NEGATIVE_FILL)
    total[...] = jnp.zeros_like(total)
    attended[...] = jnp.zeros_like(attended)

    def attend(head, keys, values, masked):
        scores = lax.dot_general(query[head], keys, (((1,), (1,)), ((), ())), preferred_element_type=f32)
        scores = masked(scores)
        before = high[head]
        after = jnp.maximum(before, jnp.max(scores, axis=1, keepdims=True))
        high[head] = after
        scale = jnp.exp(before - after)
        exponent = jnp.exp(scores - after[:, :1])
        total[head] = total[head] * scale + jnp.sum(exponent, axis=1, keepdims=True)
        attended[head] = attended[head] * scale + jnp.dot(
            exponent.astype(bf16), values, preferred_element_type=f32)

    def attend_block(i):
        mask = kv[i, pl.ds(2 * slots, MASK_ROWS), :].astype(f32)
        row = jnp.concatenate([mask[r:r + 1] for r in range(slots // E)], axis=1)

        @pl.loop(0, group)
        def _(head):
            attend(head, kv[i, pl.ds(0, slots), :], kv[i, pl.ds(slots, slots), :], lambda s: s + row)

    attend_block(me)
    remote(fresh.at[1 - core], fresh.at[1 - core], share_send, share_recv.at[1 - core], other).wait_recv()

    @pl.loop(0, group)
    def _(head):
        earlier = lax.broadcasted_iota(jnp.int32, (rows, rows), 1) <= lax.broadcasted_iota(jnp.int32, (rows, rows), 0)
        attend(head, fresh[0], fresh[1], lambda s: jnp.where(earlier, s, NEGATIVE_FILL))

    def source_chip(k):
        return index(shifted(k // 2), lax.rem(y + k, 2), 0)

    @pl.loop(1, chips)
    def _(k):
        i = source_chip(k) + core
        kv_wait(i)
        kv_on(i, k).start()
        attend_block(i)
        last = source_chip(k - 1) + 1 - core
        kv_wait(last)
        attend_block(last)

    last = source_chip(chips - 1) + 1 - core
    kv_wait(last)
    attend_block(last)

    for head in range(group):
        attention[:, head * E:(head + 1) * E] = (attended[head] / total[head]).astype(bf16)

    def product(i):
        out_weight(i).wait()
        return jnp.dot(attention[...], weights[i], preferred_element_type=f32)

    def one(slot):
        return remote(first_out.at[slot], first_in.at[slot], one_send.at[slot], one_recv.at[slot], other)

    def two(zz):
        return remote(second_out.at[zz], second_in.at[zz], two_send.at[zz], two_recv.at[zz], y_peer)

    def three(zz):
        return remote(third_out.at[zz], third_in.at[z], three_send.at[zz], three_recv.at[z], index(zz, y, core))

    def first_step(yy):
        @pl.loop(1, n_z + 1)
        def _(kz):
            zz = shifted(kz)
            slot = zz * 2 + yy
            first_out[slot] = product(index(zz, yy, 1 - core)).astype(bf16)
            one(slot).start()

    first_step(1 - y)

    @pl.loop(1, n_z + 1)
    def _(kz):
        zz = shifted(kz)
        slot = zz * 2 + 1 - y
        value = product(index(zz, 1 - y, core))
        one(slot).wait_recv()
        second_out[zz] = (value + first_in[slot].astype(f32)).astype(bf16)
        two(zz).start()

    first_step(y)

    def summed(zz):
        slot = zz * 2 + y
        value = product(index(zz, y, core))
        one(slot).wait_recv()
        value += first_in[slot].astype(f32)
        two(zz).wait_recv()
        return value + second_in[zz].astype(f32)

    @pl.loop(1, n_z)
    def _(kz):
        zz = shifted(kz)
        third_out[zz] = summed(zz).astype(bf16)
        three(zz).start()

    projected[...] = summed(z)
    for kz in range(1, n_z):
        zz = shifted(kz)
        remote(third_out.at[zz], third_in.at[zz], three_send.at[zz], three_recv.at[zz], other).wait_recv()
        projected[...] += third_in[zz].astype(f32)
    out[...] = projected[...].astype(bf16)

    for copy in sends:
        copy.wait_send()
    pair.wait_send()
    share.wait_send()
    for copy in fresh_copies:
        copy.wait_send()
    for k in range(1, chips):
        kv_to(k).wait_send()
    for k in range(chips):
        kv_on(me, k).wait_send()
    for slot in range(chips):
        one(slot).wait_send()
    for zz in range(n_z):
        two(zz).wait_send()
    for kz in range(1, n_z):
        three(shifted(kz)).wait_send()


def fused(tokens, w_query, w_key_value, w_out, cache_keys, cache_values, lengths, offset):
    devices = lax.axis_size("seq")
    rows, width = tokens.shape
    slots, kv_columns = cache_keys.shape
    n_z = devices // 4
    chips = devices // 2
    group = width // E
    f32, bf16 = jnp.float32, jnp.bfloat16
    any_space = pl.BlockSpec(memory_space=pl.ANY)
    smem = pl.BlockSpec(memory_space=pltpu.SMEM)
    vmem = pltpu.VMEM
    dma = pltpu.SemaphoreType.DMA
    block = 2 * slots + MASK_ROWS
    scratch = [
        vmem((devices, rows, width), bf16),
        vmem((devices, width, width), bf16),
        vmem(w_key_value.shape, bf16),
        vmem((chips, block, E), bf16),
        vmem((devices, block, E), bf16),
        vmem((rows, kv_columns), f32),
        vmem((2, rows, kv_columns), f32),
        vmem((chips, rows, E), bf16),
        vmem((chips, rows, E), bf16),
        vmem((2, rows, E), bf16),
        vmem((rows, width), f32),
        vmem((group, rows, E), bf16),
        vmem((group, rows, E), f32),
        vmem((group, rows, E), f32),
        vmem((group, rows, E), f32),
        vmem((rows, width), bf16),
        vmem((chips, rows, width), bf16),
        vmem((chips, rows, width), bf16),
        vmem((n_z, rows, width), bf16),
        vmem((n_z, rows, width), bf16),
        vmem((n_z, rows, width), bf16),
        vmem((n_z, rows, width), bf16),
        dma((4 + 2 * chips,)),
        dma((devices,)),
        dma((4 * n_z,)),
        dma((devices,)),
        dma((chips,)),
        dma((devices,)),
        dma((chips,)),
        dma,
        dma,
        dma((chips,)),
        dma((chips,)),
        dma,
        dma((2,)),
        dma((chips,)),
        dma((chips,)),
        dma((n_z,)),
        dma((n_z,)),
        dma((n_z,)),
        dma((n_z,)),
    ]
    return pl.pallas_call(
        kernel,
        out_shape=jax.ShapeDtypeStruct((rows, width), bf16),
        in_specs=[any_space] * 6 + [smem] * 2,
        out_specs=pl.BlockSpec(memory_space=pltpu.VMEM),
        scratch_shapes=scratch,
        compiler_params=pltpu.CompilerParams(
            collective_id=0, has_side_effects=True, vmem_limit_bytes=58 * 1024 * 1024),
        cost_estimate=pl.CostEstimate(flops=10 ** 10, bytes_accessed=45 * 10 ** 6, transcendentals=6 * 10 ** 6),
    )(tokens, w_query, w_key_value, w_out, cache_keys, cache_values, lengths, offset)


def local(tokens, w_query, w_key_value, w_out, cache_keys, cache_values, lengths, offset):
    devices = lax.axis_size("seq")
    own_index = lax.axis_index("seq")
    span_rows = tokens.shape[0]
    kv_columns = cache_keys.shape[1]
    kv_heads = kv_columns // E
    cache_rows = cache_keys.shape[0]
    token_index = jnp.arange(span_rows, dtype=jnp.int32)
    projected = jnp.dot(
        lax.all_gather(tokens, "seq", axis=1, tiled=True),
        w_query,
        preferred_element_type=jnp.float32,
    )
    local_queries = (projected * E ** (-0.5)).astype(jnp.bfloat16)
    queries = lax.all_gather(local_queries, "seq", axis=1, tiled=True)
    heads_all = queries.shape[1] // E
    group_size = heads_all // kv_heads
    summed_rows = lax.psum(jnp.dot(tokens, w_key_value, preferred_element_type=jnp.float32), "seq")
    fresh_rows = summed_rows.astype(jnp.bfloat16)
    fresh_index = jnp.arange(span_rows, dtype=jnp.int32)
    fresh_live = jnp.broadcast_to(own_index == devices - 1, (span_rows,))
    all_keys = jnp.concatenate([cache_keys, fresh_rows[:, :kv_columns]], 0)
    all_values = jnp.concatenate([cache_values, fresh_rows[:, kv_columns:]], 0)
    cache_slot = jnp.arange(cache_rows, dtype=jnp.int32)
    cache_live = (cache_slot < lengths[0]) & (own_index * cache_rows + cache_slot < offset[0])
    fresh_seen = (fresh_index[None, :] <= token_index[:, None]) & fresh_live[None, :]
    visible = jnp.concatenate(
        [jnp.broadcast_to(cache_live[None, :], (span_rows, cache_rows)), fresh_seen], 1
    )
    query_heads = queries.reshape(span_rows, kv_heads, group_size, E)
    key_heads = all_keys.reshape(-1, kv_heads, E)
    value_heads = all_values.reshape(-1, kv_heads, E)
    scores = jnp.einsum(
        "qhge,phe->hgqp", query_heads, key_heads, preferred_element_type=jnp.float32
    )
    scores = jnp.where(visible, scores, NEGATIVE_FILL)
    local_highest = jnp.max(scores, axis=-1)
    highest = lax.pmax(local_highest, "seq")
    exponent = jnp.where(visible, jnp.exp(scores - highest[..., None]), 0.0)
    local_totals = jnp.sum(exponent, axis=-1)
    weights = exponent.astype(jnp.bfloat16)
    numerator = jnp.einsum(
        "hgqp,phe->qhge", weights, value_heads, preferred_element_type=jnp.float32
    ).reshape(span_rows, heads_all * E)
    totals = lax.psum(local_totals, "seq")
    per_column = jnp.repeat(totals.reshape(heads_all, span_rows).T, E, axis=1)
    summed = lax.psum_scatter(numerator, "seq", scatter_dimension=1, tiled=True)
    col_count = summed.shape[1]
    divisor = lax.dynamic_slice_in_dim(per_column, own_index * col_count, col_count, 1)
    attention = (summed / divisor).astype(jnp.bfloat16)
    output_sum = lax.psum_scatter(
        jnp.dot(attention, w_out, preferred_element_type=jnp.float32),
        "seq",
        scatter_dimension=1,
        tiled=True,
    )
    return output_sum.astype(jnp.bfloat16)


def solution(mesh):
    in_specs = (
        P("rep", "seq"),
        P(None, "seq"),
        P("seq", None),
        P("seq", None),
        P(("rep", "seq"), None),
        P(("rep", "seq"), None),
        P(("rep", "seq")),
        P("rep"),
    )
    out_specs = P("rep", "seq")
    devices = mesh.shape["seq"]

    def body(tokens, w_query, w_key_value, w_out, cache_keys, cache_values, lengths, offset):
        kv_heads = cache_keys.shape[1] // E
        chip_per_head = devices == 2 * kv_heads and devices % 4 == 0 and w_query.shape[1] % E == 0
        form = fused if chip_per_head else local
        return form(tokens, w_query, w_key_value, w_out, cache_keys, cache_values, lengths, offset)

    return jax.shard_map(body, mesh=mesh, in_specs=in_specs, out_specs=out_specs, check_vma=False)
```

```python
import jax
import jax.numpy as jnp
from jax import lax
from jax.experimental import pallas as pl
from jax.experimental.pallas import tpu as pltpu
from jax.sharding import PartitionSpec as P

E = 128
COUNT_ROWS = 16


NEGATIVE_FILL = -1e30


def kernel(tokens, w_query, w_key_value, w_out, cache_keys, cache_values, lengths, offset, out,
           tok, weights, w_kv, stage, kv, mine, theirs, fresh_out, fresh_in, fresh, projected, query,
           high, total, attended, attention, first_out, first_in, second_out, second_in, third_out, third_in,
           load_sem, weight_sem, tok_send, tok_recv, kv_send, kv_recv, kv_pass, pair_send, pair_recv,
           fresh_send, fresh_recv, share_send, share_recv, one_send, one_recv, two_send, two_recv,
           three_send, three_recv):
    rows, width = tokens.shape
    slots = cache_keys.shape[0]
    n_z = tok.shape[0] // 4
    chips = 2 * n_z
    half = w_kv.shape[1] // 2
    group = width // E
    f32, bf16 = jnp.float32, jnp.bfloat16
    me = lax.axis_index("seq")
    core = lax.rem(me, 2)
    chip = me // 2
    y = lax.rem(chip, 2)
    z = chip // 2
    other = me + 1 - 2 * core

    def index(zz, yy, cc):
        return (zz * 2 + yy) * 2 + cc

    def shifted(kz):
        return lax.rem(z + kz, n_z)

    y_peer = index(z, 1 - y, core)

    def remote(src, dst, send, recv, peer):
        return pltpu.make_async_remote_copy(
            src_ref=src, dst_ref=dst, send_sem=send, recv_sem=recv,
            device_id={"seq": peer}, device_id_type=pl.DeviceIdType.MESH)

    own_tokens = pltpu.make_async_copy(tokens, tok.at[me], load_sem.at[0])
    own_tokens.start()
    load_kv = pltpu.make_async_copy(w_key_value, w_kv, load_sem.at[1])
    load_kv.start()

    def query_weight(i):
        return pltpu.make_async_copy(
            w_query.at[pl.ds(pl.multiple_of(i * width, width), width), :], weights.at[i], weight_sem.at[i])

    def out_weight(i):
        return pltpu.make_async_copy(
            w_out.at[:, pl.ds(pl.multiple_of(i * width, width), width)], weights.at[i], weight_sem.at[i])

    stage_loads = []
    for head in range(chips):
        columns = pl.ds(head * E, E)
        for part, cache in enumerate((cache_keys, cache_values)):
            stage_loads.append(pltpu.make_async_copy(
                cache.at[:, columns], stage.at[head, pl.ds(part * slots, slots), :],
                load_sem.at[2 + 2 * head + part]))
    own_columns = pl.ds(pl.multiple_of(chip * E, E), E)
    own_loads = [
        pltpu.make_async_copy(cache.at[:, own_columns], kv.at[me, pl.ds(part * slots, slots), :],
                              load_sem.at[2 + 2 * chips + part])
        for part, cache in enumerate((cache_keys, cache_values))]
    for load in stage_loads + own_loads:
        load.start()

    @pl.loop(0, tok.shape[0])
    def _(i):
        query_weight(i).start()

    barrier = pltpu.get_barrier_semaphore()
    peers = [index(shifted(kz), yy, core) for kz in range(n_z) for yy in (y, 1 - y)][1:] + [other]
    for peer in peers:
        pl.semaphore_signal(barrier, inc=1, device_id={"seq": peer}, device_id_type=pl.DeviceIdType.MESH)
    pl.semaphore_wait(barrier, len(peers))

    def tok_copy(i, send, peer):
        return remote(tok.at[i], tok.at[i], tok_send.at[send], tok_recv.at[i], peer)

    own_tokens.wait()
    sends = []
    for kz in range(1, n_z):
        sends.append(tok_copy(me, kz - 1, index(shifted(kz), y, core)))
    sends.append(tok_copy(me, n_z - 1, y_peer))
    sends.append(tok_copy(me, 2 * n_z - 1, other))
    for copy in sends:
        copy.start()

    filled = jnp.minimum(lengths[0], offset[0] - me * slots)
    filled = jnp.minimum(jnp.maximum(filled, 0), slots)
    low = lax.rem(filled, 16)
    upper = lax.broadcasted_iota(jnp.int32, (COUNT_ROWS, E), 0) < COUNT_ROWS // 2
    count = jnp.where(upper, filled - low, low).astype(f32).astype(bf16)
    for head in range(chips):
        stage[head, pl.ds(2 * slots, COUNT_ROWS), :] = count
    kv[me, pl.ds(2 * slots, COUNT_ROWS), :] = count

    load_kv.wait()
    for part in range(2):
        product = jnp.dot(tok[me], w_kv[:, pl.ds(part * half, half)], preferred_element_type=f32)

        @pl.when(core == part)
        def _():
            mine[...] = product

        @pl.when(core != part)
        def _():
            theirs[0] = product

    pair = remote(theirs.at[0], theirs.at[1], pair_send, pair_recv, other)
    pair.start()

    projected[...] = jnp.zeros_like(projected)

    def project(i):
        query_weight(i).wait()
        projected[...] += jnp.dot(tok[i], weights[i], preferred_element_type=f32)
        out_weight(i).start()

    project(me)

    pair.wait_recv()
    for head in range(chips):
        fresh_out[head] = (mine[:, head * E:(head + 1) * E] + theirs[1, :, head * E:(head + 1) * E]).astype(bf16)
    fresh_copies = []
    for k in range(1, chips):
        to = index(shifted(k // 2), lax.rem(y + k, 2), 0) // 2
        copy = remote(fresh_out.at[to], fresh_in.at[chip], fresh_send.at[k], fresh_recv.at[chip], to * 2 + core)
        copy.start()
        fresh_copies.append(copy)

    def fwd(i, kz, second):
        if not second:
            on = tok_copy(i, n_z - 1 + kz, y_peer)
            on.start()
            sends.append(on)
        on = tok_copy(i, 2 * n_z - 1 + 2 * kz + second, other)
        on.start()
        sends.append(on)

    def tok_wait(i):
        tok_copy(i, 0, other).wait_recv()

    near = [1, n_z - 1] + list(range(2, n_z - 1))
    for kz in near:
        i = index(shifted(kz), y, core)
        tok_wait(i)
        fwd(i, kz, 0)

    for load in stage_loads + own_loads:
        load.wait()

    def kv_to(k):
        to = index(shifted(k // 2), lax.rem(y + k, 2), 0) // 2
        return remote(stage.at[to], kv.at[me], kv_send.at[k], kv_recv.at[me], to * 2 + core)

    def kv_on(i, k):
        return remote(kv.at[i], kv.at[i], kv_pass.at[k], kv_recv.at[i], other)

    def kv_wait(i):
        kv_on(i, 0).wait_recv()

    for k in range(1, chips):
        kv_to(k).start()
    kv_on(me, 0).start()

    for kz in [0] + near:
        i = index(shifted(kz), 1 - y, core)
        tok_wait(i)
        fwd(i, kz, 1)

    @pl.loop(1, n_z)
    def _(kz):
        project(index(shifted(kz), y, core))

    @pl.loop(0, n_z)
    def _(kz):
        project(index(shifted(kz), 1 - y, core))

    @pl.loop(0, chips)
    def _(k):
        i = index(shifted(k // 2), lax.rem(y + k, 2), 1 - core)
        tok_wait(i)
        project(i)

    for head in range(group):
        query[head * rows:(head + 1) * rows, :] = (projected[:, head * E:(head + 1) * E] * E ** (-0.5)).astype(bf16)

    new_rows = fresh_out[chip].astype(f32)
    for k in range(1, chips):
        source = index(shifted(k // 2), lax.rem(y + k, 2), 0) // 2
        remote(fresh_out.at[source], fresh_in.at[source], fresh_send.at[0], fresh_recv.at[source], other).wait_recv()
        new_rows += fresh_in[source].astype(f32)
    fresh[core] = new_rows.astype(bf16)
    share = remote(fresh.at[core], fresh.at[core], share_send, share_recv.at[core], other)
    share.start()

    high[...] = jnp.full_like(high, NEGATIVE_FILL)
    total[...] = jnp.zeros_like(total)
    attended[...] = jnp.zeros_like(attended)
    pack = 2 if group % 2 == 0 else 1
    span = pack * rows

    def attend(keys, values, seen):
        turned = values.T
        for part in range(group // pack):
            at = slice(part * span, (part + 1) * span)
            scores = lax.dot_general(keys, query[at, :], (((1,), (1,)), ((), ())), preferred_element_type=f32)
            scores = jnp.where(seen, scores, NEGATIVE_FILL)
            before = high[:, at]
            after = jnp.maximum(before, jnp.max(scores, axis=0, keepdims=True))
            high[:, at] = after
            scale = jnp.exp(before - after)
            exponent = jnp.exp(scores - after)
            total[:, at] = total[:, at] * scale + jnp.sum(exponent, axis=0, keepdims=True)
            attended[:, at] = attended[:, at] * scale + jnp.dot(
                turned, exponent.astype(bf16), preferred_element_type=f32)

    def attend_block(i):
        held = kv[i, pl.ds(2 * slots, COUNT_ROWS), :].astype(f32)
        filled = (held[:1] + held[COUNT_ROWS // 2:COUNT_ROWS // 2 + 1]).astype(jnp.int32)
        filled = jnp.concatenate([filled] * pack, axis=1)
        slot = lax.broadcasted_iota(jnp.int32, (slots, span), 0)
        attend(kv[i, pl.ds(0, slots), :], kv[i, pl.ds(slots, slots), :], slot < filled)

    attend_block(me)
    remote(fresh.at[1 - core], fresh.at[1 - core], share_send, share_recv.at[1 - core], other).wait_recv()

    earlier = lax.broadcasted_iota(jnp.int32, (rows, rows), 0) <= lax.broadcasted_iota(jnp.int32, (rows, rows), 1)
    attend(fresh[0], fresh[1], jnp.concatenate([earlier] * pack, axis=1))

    def source_chip(k):
        return index(shifted(k // 2), lax.rem(y + k, 2), 0)

    @pl.loop(1, chips)
    def _(k):
        i = source_chip(k) + core
        kv_wait(i)
        kv_on(i, k).start()
        attend_block(i)
        last = source_chip(k - 1) + 1 - core
        kv_wait(last)
        attend_block(last)

    last = source_chip(chips - 1) + 1 - core
    kv_wait(last)
    attend_block(last)

    for head in range(group):
        at = slice(head * rows, (head + 1) * rows)
        attention[:, head * E:(head + 1) * E] = (attended[:, at] / total[:, at]).T.astype(bf16)

    def product(i):
        out_weight(i).wait()
        return jnp.dot(attention[...], weights[i], preferred_element_type=f32)

    def one(slot):
        return remote(first_out.at[slot], first_in.at[slot], one_send.at[slot], one_recv.at[slot], other)

    def two(zz):
        return remote(second_out.at[zz], second_in.at[zz], two_send.at[zz], two_recv.at[zz], y_peer)

    def three(zz):
        return remote(third_out.at[zz], third_in.at[z], three_send.at[zz], three_recv.at[z], index(zz, y, core))

    def first_step(yy):
        @pl.loop(1, n_z + 1)
        def _(kz):
            zz = shifted(kz)
            slot = zz * 2 + yy
            first_out[slot] = product(index(zz, yy, 1 - core)).astype(bf16)
            one(slot).start()

    first_step(1 - y)

    @pl.loop(1, n_z + 1)
    def _(kz):
        zz = shifted(kz)
        slot = zz * 2 + 1 - y
        value = product(index(zz, 1 - y, core))
        one(slot).wait_recv()
        second_out[zz] = (value + first_in[slot].astype(f32)).astype(bf16)
        two(zz).start()

    first_step(y)

    def summed(zz):
        slot = zz * 2 + y
        value = product(index(zz, y, core))
        one(slot).wait_recv()
        value += first_in[slot].astype(f32)
        two(zz).wait_recv()
        return value + second_in[zz].astype(f32)

    @pl.loop(1, n_z)
    def _(kz):
        zz = shifted(kz)
        third_out[zz] = summed(zz).astype(bf16)
        three(zz).start()

    projected[...] = summed(z)
    for kz in range(1, n_z):
        zz = shifted(kz)
        remote(third_out.at[zz], third_in.at[zz], three_send.at[zz], three_recv.at[zz], other).wait_recv()
        projected[...] += third_in[zz].astype(f32)
    out[...] = projected[...].astype(bf16)

    for copy in sends:
        copy.wait_send()
    pair.wait_send()
    share.wait_send()
    for copy in fresh_copies:
        copy.wait_send()
    for k in range(1, chips):
        kv_to(k).wait_send()
    for k in range(chips):
        kv_on(me, k).wait_send()
    for slot in range(chips):
        one(slot).wait_send()
    for zz in range(n_z):
        two(zz).wait_send()
    for kz in range(1, n_z):
        three(shifted(kz)).wait_send()


def fused(tokens, w_query, w_key_value, w_out, cache_keys, cache_values, lengths, offset):
    devices = lax.axis_size("seq")
    rows, width = tokens.shape
    slots, kv_columns = cache_keys.shape
    n_z = devices // 4
    chips = devices // 2
    group = width // E
    f32, bf16 = jnp.float32, jnp.bfloat16
    any_space = pl.BlockSpec(memory_space=pl.ANY)
    smem = pl.BlockSpec(memory_space=pltpu.SMEM)
    vmem = pltpu.VMEM
    dma = pltpu.SemaphoreType.DMA
    block = 2 * slots + COUNT_ROWS
    scratch = [
        vmem((devices, rows, width), bf16),
        vmem((devices, width, width), bf16),
        vmem(w_key_value.shape, bf16),
        vmem((chips, block, E), bf16),
        vmem((devices, block, E), bf16),
        vmem((rows, kv_columns), f32),
        vmem((2, rows, kv_columns), f32),
        vmem((chips, rows, E), bf16),
        vmem((chips, rows, E), bf16),
        vmem((2, rows, E), bf16),
        vmem((rows, width), f32),
        vmem((group * rows, E), bf16),
        vmem((1, group * rows), f32),
        vmem((1, group * rows), f32),
        vmem((E, group * rows), f32),
        vmem((rows, width), bf16),
        vmem((chips, rows, width), bf16),
        vmem((chips, rows, width), bf16),
        vmem((n_z, rows, width), bf16),
        vmem((n_z, rows, width), bf16),
        vmem((n_z, rows, width), bf16),
        vmem((n_z, rows, width), bf16),
        dma((4 + 2 * chips,)),
        dma((devices,)),
        dma((4 * n_z,)),
        dma((devices,)),
        dma((chips,)),
        dma((devices,)),
        dma((chips,)),
        dma,
        dma,
        dma((chips,)),
        dma((chips,)),
        dma,
        dma((2,)),
        dma((chips,)),
        dma((chips,)),
        dma((n_z,)),
        dma((n_z,)),
        dma((n_z,)),
        dma((n_z,)),
    ]
    return pl.pallas_call(
        kernel,
        out_shape=jax.ShapeDtypeStruct((rows, width), bf16),
        in_specs=[any_space] * 6 + [smem] * 2,
        out_specs=pl.BlockSpec(memory_space=pltpu.VMEM),
        scratch_shapes=scratch,
        compiler_params=pltpu.CompilerParams(
            collective_id=0, has_side_effects=True, vmem_limit_bytes=58 * 1024 * 1024),
        cost_estimate=pl.CostEstimate(flops=10 ** 10, bytes_accessed=45 * 10 ** 6, transcendentals=6 * 10 ** 6),
    )(tokens, w_query, w_key_value, w_out, cache_keys, cache_values, lengths, offset)


def local(tokens, w_query, w_key_value, w_out, cache_keys, cache_values, lengths, offset):
    devices = lax.axis_size("seq")
    own_index = lax.axis_index("seq")
    span_rows = tokens.shape[0]
    kv_columns = cache_keys.shape[1]
    kv_heads = kv_columns // E
    cache_rows = cache_keys.shape[0]
    token_index = jnp.arange(span_rows, dtype=jnp.int32)
    projected = jnp.dot(
        lax.all_gather(tokens, "seq", axis=1, tiled=True),
        w_query,
        preferred_element_type=jnp.float32,
    )
    local_queries = (projected * E ** (-0.5)).astype(jnp.bfloat16)
    queries = lax.all_gather(local_queries, "seq", axis=1, tiled=True)
    heads_all = queries.shape[1] // E
    group_size = heads_all // kv_heads
    summed_rows = lax.psum(jnp.dot(tokens, w_key_value, preferred_element_type=jnp.float32), "seq")
    fresh_rows = summed_rows.astype(jnp.bfloat16)
    fresh_index = jnp.arange(span_rows, dtype=jnp.int32)
    fresh_live = jnp.broadcast_to(own_index == devices - 1, (span_rows,))
    all_keys = jnp.concatenate([cache_keys, fresh_rows[:, :kv_columns]], 0)
    all_values = jnp.concatenate([cache_values, fresh_rows[:, kv_columns:]], 0)
    cache_slot = jnp.arange(cache_rows, dtype=jnp.int32)
    cache_live = (cache_slot < lengths[0]) & (own_index * cache_rows + cache_slot < offset[0])
    fresh_seen = (fresh_index[None, :] <= token_index[:, None]) & fresh_live[None, :]
    visible = jnp.concatenate(
        [jnp.broadcast_to(cache_live[None, :], (span_rows, cache_rows)), fresh_seen], 1
    )
    query_heads = queries.reshape(span_rows, kv_heads, group_size, E)
    key_heads = all_keys.reshape(-1, kv_heads, E)
    value_heads = all_values.reshape(-1, kv_heads, E)
    scores = jnp.einsum(
        "qhge,phe->hgqp", query_heads, key_heads, preferred_element_type=jnp.float32
    )
    scores = jnp.where(visible, scores, NEGATIVE_FILL)
    local_highest = jnp.max(scores, axis=-1)
    highest = lax.pmax(local_highest, "seq")
    exponent = jnp.where(visible, jnp.exp(scores - highest[..., None]), 0.0)
    local_totals = jnp.sum(exponent, axis=-1)
    weights = exponent.astype(jnp.bfloat16)
    numerator = jnp.einsum(
        "hgqp,phe->qhge", weights, value_heads, preferred_element_type=jnp.float32
    ).reshape(span_rows, heads_all * E)
    totals = lax.psum(local_totals, "seq")
    per_column = jnp.repeat(totals.reshape(heads_all, span_rows).T, E, axis=1)
    summed = lax.psum_scatter(numerator, "seq", scatter_dimension=1, tiled=True)
    col_count = summed.shape[1]
    divisor = lax.dynamic_slice_in_dim(per_column, own_index * col_count, col_count, 1)
    attention = (summed / divisor).astype(jnp.bfloat16)
    output_sum = lax.psum_scatter(
        jnp.dot(attention, w_out, preferred_element_type=jnp.float32),
        "seq",
        scatter_dimension=1,
        tiled=True,
    )
    return output_sum.astype(jnp.bfloat16)


def solution(mesh):
    in_specs = (
        P("rep", "seq"),
        P(None, "seq"),
        P("seq", None),
        P("seq", None),
        P(("rep", "seq"), None),
        P(("rep", "seq"), None),
        P(("rep", "seq")),
        P("rep"),
    )
    out_specs = P("rep", "seq")
    devices = mesh.shape["seq"]

    def body(tokens, w_query, w_key_value, w_out, cache_keys, cache_values, lengths, offset):
        kv_heads = cache_keys.shape[1] // E
        chip_per_head = devices == 2 * kv_heads and devices % 4 == 0 and w_query.shape[1] % E == 0
        form = fused if chip_per_head else local
        return form(tokens, w_query, w_key_value, w_out, cache_keys, cache_values, lengths, offset)

    return jax.shard_map(body, mesh=mesh, in_specs=in_specs, out_specs=out_specs, check_vma=False)
```
